512 devices in a mesh: blk: 16 (over x_hi, y, core), wide: 32 (over x_lo, z).
Axes of the slice: x: 4 (x_hi: 2, x_lo: 2; x = x_hi * 2 + x_lo), y: 4, z: 16, core: 2. Of those that a mesh axis runs over, the one named last changes fastest.
Arguments:
- features: float32 [65536, 128], P(('blk', 'wide')), may hold values from -6 to 6
- inv_length: float32 [128], replicated, may hold values from 0.05 to 0.2
- vectors: float32 [8, 65536], P(None, ('blk', 'wide')), may hold values from -0.09375 to 0.09375
Outputs:
- product: float32 [8, 65536], P(None, ('blk', 'wide'))
The draws below stay inside these ranges and needn't reach their ends.
All inputs are finite; a program needn't handle non-finite values.
Results may differ from the reference program's by a relative error of at most 0.0016.
Values may be sent and summed in bfloat16 or wider, within the bound.
A program may use at most 64 MiB of HBM per device.

```python
import math
import jax
import jax.numpy as jnp
from jax import lax

FEAT = 128
RHS = 8
BLOCK_ROWS = 4096
NPTS = 65536


def shard_levels(stream_key, extent, shards, low, largest):
    gain, own = 1.0, jax.random.fold_in(stream_key, 6)
    for axis_at, blocks in shards:
        steps = jnp.exp(jax.random.uniform(jax.random.fold_in(own, axis_at), (blocks,), jnp.float32, low / len(shards), largest / len(shards)))
        gain = gain * jnp.repeat(steps, extent[axis_at] // blocks).reshape([-1 if axis == axis_at else 1 for axis in range(len(extent))])
    return gain


def scatter_about(stream_key, dims, width, most, split=(), kind=jnp.bfloat16):
    array = width * jax.random.normal(stream_key, dims, jnp.float32)
    if split:
        array = array * shard_levels(stream_key, dims, split, -0.22, 0.18)
    return jnp.clip(array, -most, most).astype(kind)


def setup_inputs(seed: int = 0) -> dict:
    arg_keys = jax.random.split(jax.random.key(seed), 4)
    return {
        "features": scatter_about(arg_keys[0], (NPTS, FEAT), 1.0, 6.0, ((0, 512),), jnp.float32),
        "inv_length": jnp.clip(jnp.exp(jax.random.uniform(arg_keys[1], (FEAT,), jnp.float32, math.log(0.05), math.log(0.2))), 0.05, 0.2),
        "vectors": scatter_about(arg_keys[2], (RHS, NPTS), (NPTS // 16) ** -0.5, 0.09375, ((1, 512),), jnp.float32),
    }


def kernel_tile(cols, rows, rows_norm):
    cols_norm = lax.optimization_barrier(jnp.sum(jnp.square(cols.astype(jnp.float32)), axis=1))
    inner = lax.dot_general(cols, rows, (((1,), (1,)), ((), ())), preferred_element_type=jnp.float32)
    dist2 = jnp.maximum(cols_norm[:, None] + rows_norm[None, :] - 2.0 * inner, 0.0)
    scaled_r = jnp.sqrt(5.0 * dist2)
    return (1.0 + scaled_r + scaled_r * scaled_r / 3.0) * jnp.exp(-scaled_r)

def reference(features, inv_length, vectors):
    scaled = (features * inv_length[None, :]).astype(jnp.bfloat16)
    sqnorm = lax.optimization_barrier(jnp.sum(jnp.square(scaled.astype(jnp.float32)), axis=1))
    count = NPTS // BLOCK_ROWS
    row_blocks = scaled.reshape(count, BLOCK_ROWS, FEAT)
    norm_blocks = sqnorm.reshape(count, BLOCK_ROWS)

    def one_block(pair):
        rows, rows_norm = pair
        tile = kernel_tile(scaled, rows, rows_norm)
        return jnp.dot(vectors, tile, precision=lax.Precision.HIGHEST, preferred_element_type=jnp.float32)
    result = lax.map(one_block, (row_blocks, norm_blocks))
    return jnp.transpose(result, (1, 0, 2)).reshape(RHS, NPTS)
```

```python
import jax
import jax.numpy as jnp
from jax import lax
from jax.experimental import pallas as pl
from jax.experimental.pallas import tpu as pltpu
from jax.sharding import PartitionSpec as P

MESH = pl.DeviceIdType.MESH
F32, BF16 = jnp.float32, jnp.bfloat16

PTS = 128
FEAT = 128
RHS = 8
PLACES = 16
PLANES = 16
HALF = 8
HEAD = 2 * RHS
AUG = 16
ROWS = PLACES * PTS
PART = (HALF + 1) * PTS
COLS = 2 * PTS
CHUNK = 1024

SCALE = 5.0 / 3.0
ALPHA = 3.0 / 5.0**0.5
BETA = 0.6
DECAY = -(5.0**0.5) * 1.4426950408889634
TINY = 1e-30


def step_of(tile):
    return tile * (2 * (tile % 2) - 1) if isinstance(tile, int) else tile * (2 * lax.rem(tile, 2) - 1)


def split3(value):
    high = value.astype(BF16)
    rest = value - high.astype(F32)
    mid = rest.astype(BF16)
    low = (rest - mid.astype(F32)).astype(BF16)
    return high.astype(F32), mid.astype(F32), low.astype(F32)


def matern(dist2):
    dist2 = jnp.maximum(dist2, TINY)
    r = dist2 * lax.rsqrt(dist2)
    return ((r + ALPHA) * r + BETA) * jnp.exp2(r * DECAY)


def kernel(
    feat_ref, inv_ref, vec_ref, out_ref,
    abuf, bbuf, amat, va, vam, rowacc, corr, mean, cmsg, rmsg, rrecv, crecv,
    plane_send, plane_recv, line_send, line_recv, sib_send, sib_recv, row_send, row_recv, col_send, col_recv,
):
    blk, wide = lax.axis_index("blk"), lax.axis_index("wide")
    core = lax.rem(blk, 2)
    place = (2 * lax.div(blk, HALF) + lax.div(wide, PLANES)) * 4 + lax.rem(lax.div(blk, 2), 4)
    plane = lax.rem(wide, PLANES)

    def device(dz, dp, other):
        at = lax.rem(place + dp + PLACES, PLACES)
        x, y = lax.div(at, 4), lax.rem(at, 4)
        z = lax.rem(plane + dz + PLANES, PLANES)
        c = 1 - core if other else core
        return {"blk": lax.div(x, 2) * HALF + y * 2 + c, "wide": lax.rem(x, 2) * PLANES + z}

    def plane_copy(k):
        return pltpu.make_async_remote_copy(
            src_ref=abuf.at[0], dst_ref=abuf.at[k], send_sem=plane_send.at[k], recv_sem=plane_recv.at[k],
            device_id=device(0, -k, False), device_id_type=MESH,
        )

    def line_copy(tile):
        return pltpu.make_async_remote_copy(
            src_ref=bbuf.at[0, : HEAD + FEAT, :PTS], dst_ref=bbuf.at[tile, : HEAD + FEAT, :PTS],
            send_sem=line_send.at[tile], recv_sem=line_recv.at[tile],
            device_id=device(-step_of(tile), 0, False), device_id_type=MESH,
        )

    def sib_copy(tile):
        return pltpu.make_async_remote_copy(
            src_ref=bbuf.at[tile, : HEAD + FEAT, :PTS], dst_ref=bbuf.at[tile, : HEAD + FEAT, PTS:],
            send_sem=sib_send.at[tile], recv_sem=sib_recv.at[tile],
            device_id=device(0, 0, True), device_id_type=MESH,
        )

    def row_copy(k):
        return pltpu.make_async_remote_copy(
            src_ref=rmsg.at[k], dst_ref=rrecv.at[k], send_sem=row_send.at[k], recv_sem=row_recv.at[k],
            device_id=device(0, k, False), device_id_type=MESH,
        )

    def col_copy(tile, other):
        return pltpu.make_async_remote_copy(
            src_ref=cmsg.at[tile, other], dst_ref=crecv.at[tile, other],
            send_sem=col_send.at[tile, other], recv_sem=col_recv.at[tile, other],
            device_id=device(step_of(tile), 0, other == 1), device_id_type=MESH,
        )

    barrier = pltpu.get_barrier_semaphore()
    for k in range(1, PLACES):
        pl.semaphore_signal(barrier, inc=1, device_id=device(0, k, False), device_id_type=MESH)
    for tile in range(1, HALF + 1):
        pl.semaphore_signal(barrier, inc=1, device_id=device(step_of(tile), 0, False), device_id_type=MESH)
    pl.semaphore_signal(barrier, inc=1, device_id=device(0, 0, True), device_id_type=MESH)

    scaled = (feat_ref[...] * inv_ref[...]).astype(BF16).astype(F32)
    vec = vec_ref[...]
    vec_high = vec.astype(BF16).astype(F32)
    head = jnp.concatenate([vec_high, vec - vec_high], axis=0).astype(BF16)
    abuf[0, :PTS, :] = (scaled * -2.0).astype(BF16)
    abuf[0, PTS:, :] = head
    bbuf[0, :HEAD, :PTS] = head
    bbuf[0, HEAD : HEAD + FEAT, :PTS] = scaled.T.astype(BF16)

    pl.semaphore_wait(barrier, PLACES - 1 + HALF + 1)

    sib_copy(0).start()
    for tile in range(1, HALF + 1):
        line_copy(tile).start()
    for k in range(1, PLACES):
        plane_copy(k).start()

    lane = lax.broadcasted_iota(jnp.int32, (PTS, PTS), 1)
    ones = jnp.ones((2 * FEAT, PTS), BF16)

    def add_rows(k):
        at = pl.multiple_of(k * PTS, PTS)
        points = abuf[k, :PTS, :]
        wide_points = points.astype(F32)
        square = wide_points * wide_points
        high = square.astype(BF16)
        low = (square - high.astype(F32)).astype(BF16)
        norm = 0.25 * jnp.dot(jnp.concatenate([high, low], axis=1), ones, preferred_element_type=F32)
        n0, n1, n2 = split3(norm)
        extra = jnp.where(lane == 0, n0, jnp.where(lane == 1, n1, jnp.where(lane == 2, n2, jnp.where(lane < 6, 1.0, 0.0))))
        amat[pl.ds(at, PTS), :FEAT] = points
        amat[pl.ds(at, PTS), FEAT:] = extra.astype(BF16)
        va[:, pl.ds(at, PTS)] = abuf[k, PTS:, :]

    add_rows(0)

    def arrive(k, _):
        plane_copy(k).wait_recv()
        add_rows(k)
        return 0

    lax.fori_loop(1, PLACES, arrive, 0)

    k_of = lax.div(lax.broadcasted_iota(jnp.int32, (HEAD, PART), 1), PTS)
    vam[...] = jnp.where((k_of > 0) & (k_of < HALF), va[:, :PART].astype(F32), 0.0).astype(BF16)
    mean[...] = (jnp.dot(jnp.full((HEAD, ROWS), 1.0 / ROWS, BF16), amat[...], preferred_element_type=F32)).astype(BF16)

    def both(value):
        return value[:RHS] + value[RHS:]

    sum_full = jnp.sum(both(va[...].astype(F32)), axis=1, keepdims=True)
    sum_part = jnp.sum(both(vam[...].astype(F32)), axis=1, keepdims=True)
    rowacc[...] = jnp.zeros_like(rowacc)
    corr[...] = jnp.zeros_like(corr)

    sub = lax.broadcasted_iota(jnp.int32, (AUG, COLS), 0)

    def run_tile(tile, rows, weights, weight_sum, which):
        cols = bbuf[tile, HEAD : HEAD + FEAT, :].astype(F32)
        n0, n1, n2 = split3(jnp.sum(cols * cols, axis=0, keepdims=True))
        extra = jnp.where(sub < 3, 1.0, jnp.where(sub == 3, n0, jnp.where(sub == 4, n1, jnp.where(sub == 5, n2, 0.0))))
        bbuf[tile, HEAD + FEAT :, :] = extra.astype(BF16)
        right = bbuf[tile, HEAD:, :]
        vb = bbuf[tile, :HEAD, :]
        middle = matern(jnp.dot(mean[:, : FEAT + AUG], right, preferred_element_type=F32)[:RHS])
        vb_wide = vb.astype(F32)
        corr[which] += both(vb_wide) * middle
        col = weight_sum * middle
        start = 0
        while start < rows:
            size = min(CHUNK, rows - start)
            if rows - start - size < CHUNK // 2:
                size = rows - start
            dist2 = jnp.dot(amat[start : start + size, : FEAT + AUG], right, preferred_element_type=F32)
            entry = matern(dist2).reshape(size // RHS, RHS, COLS) - middle[None]
            entry = entry.reshape(size, COLS).astype(BF16)
            rowacc[:, start : start + size] += lax.dot_general(
                vb, entry, (((1,), (1,)), ((), ())), preferred_element_type=F32
            )
            col += both(jnp.dot(weights[:, start : start + size], entry, preferred_element_type=F32))
            start += size
        cmsg[tile, 0] = col[:, :PTS]
        cmsg[tile, 1] = col[:, PTS:]

    line_copy(1).wait_recv()
    sib_copy(1).start()

    def full_tile(tile, _):
        line_copy(tile + 1).wait_recv()
        sib_copy(tile + 1).start()
        sib_copy(tile).wait_recv()
        run_tile(tile, ROWS, va, sum_full, 0)
        col_copy(tile, 0).start()
        col_copy(tile, 1).start()
        return 0

    lax.fori_loop(1, HALF, full_tile, 0)

    const_full = jnp.sum(corr[0], axis=1, keepdims=True)

    for k in range(HALF + 1, PLACES):
        rmsg[k] = both(rowacc[:, k * PTS : (k + 1) * PTS]) + const_full
        row_copy(k).start()

    sib_copy(HALF).wait_recv()
    run_tile(HALF, PART, vam, sum_part, 1)
    col_copy(HALF, 0).start()
    col_copy(HALF, 1).start()

    sib_copy(0).wait_recv()
    run_tile(0, PART, vam, sum_part, 1)
    col_copy(0, 1).start()

    const_part = const_full + jnp.sum(corr[1], axis=1, keepdims=True)
    for k in range(1, HALF + 1):
        rmsg[k] = both(rowacc[:, k * PTS : (k + 1) * PTS]) + const_part
        row_copy(k).start()

    total = both(rowacc[:, :PTS]) + const_part + cmsg[0, 0]
    for tile in range(HALF + 1):
        for other in range(2):
            if tile or other:
                col_copy(tile, other).wait_recv()
                total += crecv[tile, other]
    for k in list(range(HALF + 1, PLACES)) + list(range(1, HALF + 1)):
        row_copy(k).wait_recv()
        total += rrecv[k]
    out_ref[...] = total * SCALE

    for tile in range(HALF + 1):
        sib_copy(tile).wait_send()
        if tile:
            line_copy(tile).wait_send()
            col_copy(tile, 0).wait_send()
        col_copy(tile, 1).wait_send()
    for k in range(1, PLACES):
        plane_copy(k).wait_send()
        row_copy(k).wait_send()


def body(features, inv_length, vectors):
    dma = pltpu.SemaphoreType.DMA
    return pl.pallas_call(
        kernel,
        out_shape=jax.ShapeDtypeStruct((RHS, PTS), F32),
        in_specs=[pl.BlockSpec(memory_space=pltpu.VMEM)] * 3,
        out_specs=pl.BlockSpec(memory_space=pltpu.VMEM),
        scratch_shapes=[
            pltpu.VMEM((PLACES, PTS + HEAD, FEAT), BF16),
            pltpu.VMEM((HALF + 1, HEAD + FEAT + AUG, COLS), BF16),
            pltpu.VMEM((ROWS, 2 * FEAT), BF16),
            pltpu.VMEM((HEAD, ROWS), BF16),
            pltpu.VMEM((HEAD, PART), BF16),
            pltpu.VMEM((HEAD, ROWS), F32),
            pltpu.VMEM((2, RHS, COLS), F32),
            pltpu.VMEM((HEAD, 2 * FEAT), BF16),
            pltpu.VMEM((HALF + 1, 2, RHS, PTS), F32),
            pltpu.VMEM((PLACES, RHS, PTS), F32),
            pltpu.VMEM((PLACES, RHS, PTS), F32),
            pltpu.VMEM((HALF + 1, 2, RHS, PTS), F32),
            dma((PLACES,)), dma((PLACES,)),
            dma((HALF + 1,)), dma((HALF + 1,)),
            dma((HALF + 1,)), dma((HALF + 1,)),
            dma((PLACES,)), dma((PLACES,)),
            dma((HALF + 1, 2)), dma((HALF + 1, 2)),
        ],
        compiler_params=pltpu.CompilerParams(
            collective_id=0, has_side_effects=True, vmem_limit_bytes=48 * 2**20
        ),
        name="matern",
    )(features, inv_length.reshape(1, FEAT), vectors)


def solution(mesh):
    return jax.shard_map(
        body,
        mesh=mesh,
        in_specs=(P(("blk", "wide"), None), P(), P(None, ("blk", "wide"))),
        out_specs=P(None, ("blk", "wide")),
        check_vma=False,
    )
```

```python
import jax
import jax.numpy as jnp
from jax import lax
from jax.experimental import pallas as pl
from jax.experimental.pallas import tpu as pltpu
from jax.sharding import PartitionSpec as P

MESH = pl.DeviceIdType.MESH
F32, BF16 = jnp.float32, jnp.bfloat16

PTS = 128
FEAT = 128
RHS = 8
PLACES = 16
PLANES = 16
HALF = 8
HEAD = 2 * RHS
AUG = 16
ROWS = PLACES * PTS
PART = (HALF + 1) * PTS
COLS = 2 * PTS
NEAR_LAST = (10, 6, 9, 7, 11, 5, 14, 2, 8, 13, 3, 15, 1, 12, 4)
RELAY = 6

SCALE = 5.0 / 3.0
ALPHA = 3.0 / 5.0**0.5
BETA = 0.6
DECAY = -(5.0**0.5) * 1.4426950408889634
TINY = 1e-30


def packed(*tiles):
    return sum((tile - 1) * 8**i for i, tile in enumerate(tiles))


ORDERS = (packed(1, 2, 3, 4, 6, 5, 7, 8), packed(6, 8, 7, 5, 1, 2, 3, 4), packed(4, 3, 1, 2, 8, 7, 6, 5))


def step_of(tile):
    return tile * (1 - 2 * ((tile + 3) // 8))


def split3(value):
    high = value.astype(BF16)
    rest = value - high.astype(F32)
    mid = rest.astype(BF16)
    low = (rest - mid.astype(F32)).astype(BF16)
    return high.astype(F32), mid.astype(F32), low.astype(F32)


def matern(dist2):
    dist2 = jnp.maximum(dist2, TINY)
    r = dist2 * lax.rsqrt(dist2)
    return ((r + ALPHA) * r + BETA) * jnp.exp2(r * DECAY)


def kernel(
    feat_hbm, inv_hbm, vec_hbm, out_ref,
    feat_ref, inv_ref, vec_ref, abuf, bbuf, amat, va, rowacc, corr, mean, mid, wsum, colacc, cmsg, rmsg, rrecv, crecv,
    in_sem, plane_send, plane_recv, line_send, line_recv, sib_send, sib_recv, row_send, row_recv, col_send, col_recv,
):
    loads = [
        pltpu.make_async_copy(src, dst, in_sem.at[i])
        for i, (src, dst) in enumerate(((feat_hbm, feat_ref), (inv_hbm, inv_ref), (vec_hbm, vec_ref)))
    ]
    for load in loads:
        load.start()

    blk, wide = lax.axis_index("blk"), lax.axis_index("wide")
    core = lax.rem(blk, 2)
    place = (2 * lax.div(blk, HALF) + lax.div(wide, PLANES)) * 4 + lax.rem(lax.div(blk, 2), 4)
    plane = lax.rem(wide, PLANES)

    def device(dz, dp, other):
        at = lax.rem(place + dp + PLACES, PLACES)
        x, y = lax.div(at, 4), lax.rem(at, 4)
        z = lax.rem(plane + dz + PLANES, PLANES)
        c = 1 - core if other else core
        return {"blk": lax.div(x, 2) * HALF + y * 2 + c, "wide": lax.rem(x, 2) * PLANES + z}

    def plane_copy(k):
        return pltpu.make_async_remote_copy(
            src_ref=abuf.at[0], dst_ref=abuf.at[k], send_sem=plane_send.at[k], recv_sem=plane_recv.at[k],
            device_id=device(0, -k, False), device_id_type=MESH,
        )

    def line_copy(tile, source=0, hops=0):
        return pltpu.make_async_remote_copy(
            src_ref=bbuf.at[source, : HEAD + FEAT, :PTS], dst_ref=bbuf.at[tile, : HEAD + FEAT, :PTS],
            send_sem=line_send.at[tile], recv_sem=line_recv.at[tile],
            device_id=device(hops, 0, False), device_id_type=MESH,
        )

    def sib_copy(tile):
        return pltpu.make_async_remote_copy(
            src_ref=bbuf.at[tile, : HEAD + FEAT, :PTS], dst_ref=bbuf.at[tile, : HEAD + FEAT, PTS:],
            send_sem=sib_send.at[tile], recv_sem=sib_recv.at[tile],
            device_id=device(0, 0, True), device_id_type=MESH,
        )

    def row_copy(k):
        return pltpu.make_async_remote_copy(
            src_ref=rmsg.at[k], dst_ref=rrecv.at[k], send_sem=row_send.at[k], recv_sem=row_recv.at[k],
            device_id=device(0, k, False), device_id_type=MESH,
        )

    def col_copy(tile, other):
        return pltpu.make_async_remote_copy(
            src_ref=cmsg.at[tile, other], dst_ref=crecv.at[tile, other],
            send_sem=col_send.at[tile, other], recv_sem=col_recv.at[tile, other],
            device_id=device(step_of(tile), 0, other == 1), device_id_type=MESH,
        )

    barrier = pltpu.get_barrier_semaphore()
    for dz in (-RELAY, 2, -2, 1, -1):
        pl.semaphore_signal(barrier, inc=1, device_id=device(dz, 0, False), device_id_type=MESH)
    for k in NEAR_LAST:
        pl.semaphore_signal(barrier, inc=1, device_id=device(0, k, False), device_id_type=MESH)
    pl.semaphore_signal(barrier, inc=1, device_id=device(0, 0, True), device_id_type=MESH)

    for load in loads:
        load.wait()
    scaled = (feat_ref[...] * inv_ref[...]).astype(BF16).astype(F32)
    vec = vec_ref[...]
    vec_high = vec.astype(BF16).astype(F32)
    head = jnp.concatenate([vec_high, vec - vec_high], axis=0).astype(BF16)
    abuf[0, :PTS, :] = (scaled * -2.0).astype(BF16)
    abuf[0, PTS:, :] = head
    bbuf[0, :HEAD, :PTS] = head
    bbuf[0, HEAD : HEAD + FEAT, :PTS] = scaled.T.astype(BF16)

    pl.semaphore_wait(barrier, PLACES - 1 + 5 + 1)

    line_copy(RELAY, 0, RELAY).start()
    line_copy(2, 0, -2).start()
    line_copy(1, 0, -1).start()
    sib_copy(0).start()
    for k in range(1, PLACES):
        plane_copy(k).start()

    lane = lax.broadcasted_iota(jnp.int32, (PTS, PTS), 1)
    ones = jnp.ones((2 * FEAT, PTS), BF16)

    def add_rows(k):
        at = pl.multiple_of(k * PTS, PTS)
        points = abuf[k, :PTS, :]
        wide_points = points.astype(F32)
        square = wide_points * wide_points
        high = square.astype(BF16)
        low = (square - high.astype(F32)).astype(BF16)
        norm = 0.25 * jnp.dot(jnp.concatenate([high, low], axis=1), ones, preferred_element_type=F32)
        n0, n1, n2 = split3(norm)
        extra = jnp.where(lane == 0, n0, jnp.where(lane == 1, n1, jnp.where(lane == 2, n2, jnp.where(lane < 6, 1.0, 0.0))))
        amat[pl.ds(at, PTS), :FEAT] = points
        amat[pl.ds(at, PTS), FEAT:] = extra.astype(BF16)
        va[0, :, pl.ds(at, PTS)] = abuf[k, PTS:, :]

    def arrive(k, _):
        plane_copy(k).wait_recv()
        add_rows(k)
        return 0

    add_rows(0)
    rowacc[...] = jnp.zeros_like(rowacc)
    corr[...] = jnp.zeros_like(corr)
    lax.fori_loop(1, 5, arrive, 0)
    line_copy(1).wait_recv()
    sib_copy(1).start()
    line_copy(2).wait_recv()
    line_copy(4, 2, -2).start()
    line_copy(3, 2, -1).start()
    sib_copy(2).start()
    lax.fori_loop(5, HALF + 1, arrive, 0)

    def both(value):
        return value[:RHS] + value[RHS:]

    k_of = lax.div(lax.broadcasted_iota(jnp.int32, (HEAD, PART), 1), PTS)
    masked = jnp.where((k_of > 0) & (k_of < HALF), va[0, :, :PART].astype(F32), 0.0)
    va[1, :, :PART] = masked.astype(BF16)

    def spread(value):
        return jnp.broadcast_to(jnp.sum(both(value), axis=1, keepdims=True), (RHS, COLS))

    wsum[0] = spread(va[0, :, :PART].astype(F32))
    wsum[1] = spread(masked)
    mean[...] = jnp.dot(jnp.full((HEAD, PART), 1.0 / PART, BF16), amat[:PART], preferred_element_type=F32).astype(BF16)

    sub = lax.broadcasted_iota(jnp.int32, (AUG, COLS), 0)

    def add_columns(tile):
        cols = bbuf[tile, HEAD : HEAD + FEAT, :].astype(F32)
        n0, n1, n2 = split3(jnp.sum(cols * cols, axis=0, keepdims=True))
        extra = jnp.where(sub < 3, 1.0, jnp.where(sub == 3, n0, jnp.where(sub == 4, n1, jnp.where(sub == 5, n2, 0.0))))
        bbuf[tile, HEAD + FEAT :, :] = extra.astype(BF16)
        mid[tile] = matern(jnp.dot(mean[:, : FEAT + AUG], bbuf[tile, HEAD:, :], preferred_element_type=F32)[:RHS])

    def run_part(tile, first, last, weights):
        middle = mid[tile]
        vb = bbuf[tile, :HEAD, :]
        if first == 0:
            corr[0] += both(vb.astype(F32)) * middle
        if last == ROWS:
            corr[1] += both(vb.astype(F32)) * middle
        dist2 = jnp.dot(amat[first:last, : FEAT + AUG], bbuf[tile, HEAD:, :], preferred_element_type=F32)
        entry = matern(dist2).reshape((last - first) // RHS, RHS, COLS) - middle[None]
        entry = entry.reshape(last - first, COLS).astype(BF16)
        rowacc[:, first:last] += lax.dot_general(vb, entry, (((1,), (1,)), ((), ())), preferred_element_type=F32)
        return both(jnp.dot(weights, entry, preferred_element_type=F32))

    def first_part(tile):
        kind = (HALF - lax.rem(tile, HALF)) // HALF
        add_columns(tile)
        colacc[tile] = run_part(tile, 0, PART, va[kind, :, :PART]) + wsum[kind] * mid[tile]

    def second_part(tile):
        colacc[tile] += run_part(tile, PART, ROWS, va[0, :, PART:]) + wsum[2] * mid[tile]

    def whole_tile(tile):
        add_columns(tile)
        colacc[tile] = run_part(tile, 0, ROWS, va[0]) + (wsum[0] + wsum[2]) * mid[tile]

    def send_columns(tile):
        total = colacc[tile]
        cmsg[tile, 0] = total[:, :PTS]
        cmsg[tile, 1] = total[:, PTS:]
        col_copy(tile, 0).start()
        col_copy(tile, 1).start()

    def send_rows(ks, part):
        const = jnp.sum(corr[part], axis=1, keepdims=True)
        for k in ks:
            rmsg[k] = both(rowacc[:, k * PTS : (k + 1) * PTS]) + const
            if k:
                row_copy(k).start()

    def fetch(tile):
        line_copy(tile).wait_recv()
        sib_copy(tile).start()

    def slot(index, order):
        late = index > 2
        tile = lax.select(late, lax.rem(order, 8) + 1, index)
        order = lax.select(late, order // 8, order)
        after = lax.rem(order, 8) + 1

        @pl.when(index == 1)
        def _():
            line_copy(RELAY).wait_recv()
            line_copy(8, RELAY, 2).start()
            line_copy(7, RELAY, 1).start()
            line_copy(5, RELAY, -1).start()
            sib_copy(RELAY).start()

        @pl.when(index == 3)
        def _():
            lax.fori_loop(HALF + 1, PLACES, arrive, 0)
            wsum[2] = spread(va[0, :, PART:].astype(F32))

        @pl.when((index > 1) & (index < 10) & (after > 2) & (after != RELAY))
        def _():
            fetch(after)

        @pl.when((index < 3) | (tile > 2))
        def _():
            sib_copy(tile).wait_recv()

        @pl.when((index < 3) | (tile == HALF))
        def _():
            first_part(tile)

        @pl.when(late & (tile < 3))
        def _():
            second_part(tile)

        @pl.when(late & (tile > 2) & (tile < HALF))
        def _():
            whole_tile(tile)

        @pl.when(late)
        def _():
            send_columns(tile)

        return order

    third, quarter = lax.div(plane, 8), lax.div(plane, 12)
    order = ORDERS[0] + third * (ORDERS[1] - ORDERS[0]) + quarter * (ORDERS[2] - ORDERS[1])
    lax.fori_loop(0, 11, slot, order)

    send_rows(range(HALF + 1), 0)
    send_rows(range(HALF + 1, PLACES), 1)
    cmsg[0, 1] = colacc[0, :, PTS:]
    col_copy(0, 1).start()

    total = rmsg[0] + colacc[0, :, :PTS]
    for tile in range(HALF + 1):
        for other in range(2):
            if tile or other:
                col_copy(tile, other).wait_recv()
                total += crecv[tile, other]
    for k in range(1, PLACES):
        row_copy(k).wait_recv()
        total += rrecv[k]
    out_ref[...] = total * SCALE

    for tile in range(HALF + 1):
        sib_copy(tile).wait_send()
        if tile:
            line_copy(tile).wait_send()
            col_copy(tile, 0).wait_send()
        col_copy(tile, 1).wait_send()
    for k in range(1, PLACES):
        plane_copy(k).wait_send()
        row_copy(k).wait_send()


def body(features, inv_length, vectors):
    dma = pltpu.SemaphoreType.DMA
    return pl.pallas_call(
        kernel,
        out_shape=jax.ShapeDtypeStruct((RHS, PTS), F32),
        in_specs=[pl.BlockSpec(memory_space=pltpu.HBM)] * 3,
        out_specs=pl.BlockSpec(memory_space=pltpu.VMEM),
        scratch_shapes=[
            pltpu.VMEM((PTS, FEAT), F32),
            pltpu.VMEM((1, FEAT), F32),
            pltpu.VMEM((RHS, PTS), F32),
            pltpu.VMEM((PLACES, PTS + HEAD, FEAT), BF16),
            pltpu.VMEM((HALF + 1, HEAD + FEAT + AUG, COLS), BF16),
            pltpu.VMEM((ROWS, 2 * FEAT), BF16),
            pltpu.VMEM((2, HEAD, ROWS), BF16),
            pltpu.VMEM((HEAD, ROWS), F32),
            pltpu.VMEM((2, RHS, COLS), F32),
            pltpu.VMEM((HEAD, 2 * FEAT), BF16),
            pltpu.VMEM((HALF + 1, RHS, COLS), F32),
            pltpu.VMEM((3, RHS, COLS), F32),
            pltpu.VMEM((HALF + 1, RHS, COLS), F32),
            pltpu.VMEM((HALF + 1, 2, RHS, PTS), F32),
            pltpu.VMEM((PLACES, RHS, PTS), F32),
            pltpu.VMEM((PLACES, RHS, PTS), F32),
            pltpu.VMEM((HALF + 1, 2, RHS, PTS), F32),
            dma((3,)),
            dma((PLACES,)), dma((PLACES,)),
            dma((HALF + 1,)), dma((HALF + 1,)),
            dma((HALF + 1,)), dma((HALF + 1,)),
            dma((PLACES,)), dma((PLACES,)),
            dma((HALF + 1, 2)), dma((HALF + 1, 2)),
        ],
        compiler_params=pltpu.CompilerParams(
            collective_id=0, has_side_effects=True, vmem_limit_bytes=60 * 2**20
        ),
        name="matern",
    )(features, inv_length.reshape(1, FEAT), vectors)


def solution(mesh):
    return jax.shard_map(
        body,
        mesh=mesh,
        in_specs=(P(("blk", "wide"), None), P(), P(None, ("blk", "wide"))),
        out_specs=P(None, ("blk", "wide")),
        check_vma=False,
    )
```

```python
import jax
import jax.numpy as jnp
from jax import lax
from jax.experimental import pallas as pl
from jax.experimental.pallas import tpu as pltpu
from jax.sharding import PartitionSpec as P

MESH = pl.DeviceIdType.MESH
F32, BF16 = jnp.float32, jnp.bfloat16

PTS = 128
FEAT = 128
RHS = 8
PLANES = 16
HALF = 8
HEAD = 2 * RHS
AUG = 16
COLS = 2 * PTS
RELAY = 6

SLOTS = (
    (0, 0), (1, 0), (0, 1), (1, 1), (1, -1), (-1, 0), (0, -1), (-1, -1), (-1, 1),
    (2, 0), (0, 2), (2, 2), (1, 2), (2, 1), (-1, 2), (2, -1),
)
PLACES = len(SLOTS)
NEAR = 9
LONE = (0, 9, 10, 11)
PASSED = ((11, 7, (-1, -1)), (15, 7, (-1, 0)), (14, 7, (0, -1)), (13, 3, (1, 0)), (12, 3, (0, 1)), (9, 1, (1, 0)), (10, 2, (0, 1)))
ROWS = PLACES * PTS
PART = NEAR * PTS
ENDS = (5 * PTS, 14 * PTS)


def packed(*tiles):
    return sum(tile * 9**i for i, tile in enumerate(tiles))


ORDERS = (packed(1, 2, 3, 4, 6, 5, 7, 8, 0), packed(1, 2, 6, 8, 7, 5, 3, 4, 0), packed(1, 2, 6, 5, 7, 8, 3, 4, 0))

SCALE = 5.0 / 3.0
ALPHA = 3.0 / 5.0**0.5
BETA = 0.6
DECAY = -(5.0**0.5) * 1.4426950408889634
TINY = 1e-30


def step_of(tile):
    return tile * (2 * ((tile + 3) // 8) - 1)


def split3(value):
    high = value.astype(BF16)
    rest = value - high.astype(F32)
    mid = rest.astype(BF16)
    low = (rest - mid.astype(F32)).astype(BF16)
    return high.astype(F32), mid.astype(F32), low.astype(F32)


def matern(dist2):
    r = dist2 * lax.rsqrt(dist2)
    return ((r + ALPHA) * r + BETA) * jnp.exp2(r * DECAY)


def kernel(
    feat_hbm, inv_hbm, vec_hbm, out_ref,
    feat_ref, inv_ref, vec_ref, abuf, bbuf, amat, va, rowacc, corr, work, mean, mid, wsum, colacc, cmsg, rmsg, rrecv, crecv,
    in_sem, plane_send, plane_recv, line_send, line_recv, sib_send, sib_recv, row_send, row_recv, col_send, col_recv,
):
    loads = [
        pltpu.make_async_copy(src, dst, in_sem.at[i])
        for i, (src, dst) in enumerate(((feat_hbm, feat_ref), (inv_hbm, inv_ref), (vec_hbm, vec_ref)))
    ]
    for load in loads:
        load.start()

    blk, wide = lax.axis_index("blk"), lax.axis_index("wide")
    core = lax.rem(blk, 2)
    x_here = 2 * lax.div(blk, HALF) + lax.div(wide, PLANES)
    y_here = lax.rem(lax.div(blk, 2), 4)
    plane = lax.rem(wide, PLANES)

    def device(dz, offset, other):
        x, y = lax.rem(x_here + offset[0] + 4, 4), lax.rem(y_here + offset[1] + 4, 4)
        z = lax.rem(plane + dz + PLANES, PLANES)
        c = 1 - core if other else core
        return {"blk": lax.div(x, 2) * HALF + y * 2 + c, "wide": lax.rem(x, 2) * PLANES + z}

    def back(offset):
        return (-offset[0], -offset[1])

    def plane_copy(k, source=0, offset=(0, 0)):
        return pltpu.make_async_remote_copy(
            src_ref=abuf.at[source], dst_ref=abuf.at[k], send_sem=plane_send.at[k], recv_sem=plane_recv.at[k],
            device_id=device(0, offset, False), device_id_type=MESH,
        )

    def pass_on(source):
        for k, at, offset in PASSED:
            if at == source:
                plane_copy(k, source, back(offset)).start()

    def line_copy(tile, source=0, hops=0):
        return pltpu.make_async_remote_copy(
            src_ref=bbuf.at[source, : HEAD + FEAT, :PTS], dst_ref=bbuf.at[tile, : HEAD + FEAT, :PTS],
            send_sem=line_send.at[tile], recv_sem=line_recv.at[tile],
            device_id=device(hops, (0, 0), False), device_id_type=MESH,
        )

    def sib_copy(tile):
        return pltpu.make_async_remote_copy(
            src_ref=bbuf.at[tile, : HEAD + FEAT, :PTS], dst_ref=bbuf.at[tile, : HEAD + FEAT, PTS:],
            send_sem=sib_send.at[tile], recv_sem=sib_recv.at[tile],
            device_id=device(0, (0, 0), True), device_id_type=MESH,
        )

    def row_copy(k):
        return pltpu.make_async_remote_copy(
            src_ref=rmsg.at[k], dst_ref=rrecv.at[k], send_sem=row_send.at[k], recv_sem=row_recv.at[k],
            device_id=device(0, SLOTS[k], False), device_id_type=MESH,
        )

    def col_copy(tile, other):
        return pltpu.make_async_remote_copy(
            src_ref=cmsg.at[tile, other], dst_ref=crecv.at[tile, other],
            send_sem=col_send.at[tile, other], recv_sem=col_recv.at[tile, other],
            device_id=device(step_of(tile), (0, 0), other == 1), device_id_type=MESH,
        )

    barrier = pltpu.get_barrier_semaphore()
    for dz in (RELAY, 2, -2, 1, -1):
        pl.semaphore_signal(barrier, inc=1, device_id=device(dz, (0, 0), False), device_id_type=MESH)
    for k in range(1, NEAR):
        pl.semaphore_signal(barrier, inc=1, device_id=device(0, SLOTS[k], False), device_id_type=MESH)
    pl.semaphore_signal(barrier, inc=1, device_id=device(0, (0, 0), True), device_id_type=MESH)

    for load in loads:
        load.wait()
    scaled = (feat_ref[...] * inv_ref[...]).astype(BF16).astype(F32)
    vec = vec_ref[...]
    vec_high = vec.astype(BF16).astype(F32)
    head = jnp.concatenate([vec_high, vec - vec_high], axis=0).astype(BF16)
    abuf[0, :PTS, :] = (scaled * -2.0).astype(BF16)
    abuf[0, PTS:, :] = head
    bbuf[0, :HEAD, :PTS] = head
    bbuf[0, HEAD : HEAD + FEAT, :PTS] = scaled.T.astype(BF16)

    pl.semaphore_wait(barrier, NEAR - 1 + 5 + 1)

    line_copy(RELAY, 0, -RELAY).start()
    line_copy(2, 0, 2).start()
    for k in (7, 3, 1, 2):
        plane_copy(k, 0, back(SLOTS[k])).start()
    line_copy(1, 0, 1).start()
    sib_copy(0).start()
    for k in (4, 5, 6, 8):
        plane_copy(k, 0, back(SLOTS[k])).start()

    lane = lax.broadcasted_iota(jnp.int32, (PTS, PTS), 1)
    ones = jnp.ones((2 * FEAT, PTS), BF16)

    def add_rows(k):
        at = k * PTS
        points = abuf[k, :PTS, :]
        wide_points = points.astype(F32)
        square = wide_points * wide_points
        high = square.astype(BF16)
        low = (square - high.astype(F32)).astype(BF16)
        norm = 0.25 * jnp.dot(jnp.concatenate([high, low], axis=1), ones, preferred_element_type=F32)
        n0, n1, n2 = split3(norm)
        extra = jnp.where(lane == 0, n0, jnp.where(lane == 1, n1, jnp.where(lane == 2, n2, jnp.where(lane < 6, 1.0, 0.0))))
        amat[at : at + PTS, :FEAT] = points
        amat[at : at + PTS, FEAT:] = extra.astype(BF16)
        va[0, :, at : at + PTS] = abuf[k, PTS:, :]

    def fetch(tile):
        line_copy(tile).wait_recv()
        sib_copy(tile).start()

    add_rows(0)
    rowacc[...] = jnp.zeros_like(rowacc)
    corr[...] = jnp.zeros_like(corr)
    for k in (7, 3, 1, 2):
        plane_copy(k).wait_recv()
        pass_on(k)
    for k in (7, 3, 1, 2):
        add_rows(k)
    fetch(1)
    fetch(2)
    line_copy(4, 2, 2).start()
    line_copy(3, 2, 1).start()
    for k in (4, 5, 6, 8):
        plane_copy(k).wait_recv()
    for k in (4, 5, 6, 8):
        add_rows(k)

    def both(value):
        return value[:RHS] + value[RHS:]

    def spread(value):
        return jnp.broadcast_to(jnp.sum(both(value), axis=1, keepdims=True), (RHS, COLS))

    wsum[0] = spread(va[0, :, :PART].astype(F32))
    mean[...] = jnp.dot(jnp.full((HEAD, PART), 1.0 / PART, BF16), amat[:PART], preferred_element_type=F32).astype(BF16)

    sub = lax.broadcasted_iota(jnp.int32, (AUG, COLS), 0)

    def add_columns(tile):
        cols = bbuf[tile, HEAD : HEAD + FEAT, :].astype(F32)
        n0, n1, n2 = split3(jnp.sum(cols * cols, axis=0, keepdims=True))
        extra = jnp.where(sub < 3, 1.0, jnp.where(sub == 3, n0, jnp.where(sub == 4, n1, jnp.where(sub == 5, n2, 0.0))))
        bbuf[tile, HEAD + FEAT :, :] = extra.astype(BF16)
        mid[tile] = matern(jnp.maximum(jnp.dot(mean[:, : FEAT + AUG], bbuf[tile, HEAD:, :], preferred_element_type=F32)[:RHS], TINY))

    def run_part(tile, first, last, kind):
        right = bbuf[tile, HEAD:, :]
        dist2 = jnp.dot(amat[first:last, : FEAT + AUG], right, preferred_element_type=F32)
        work[first:last] = jnp.maximum(dist2, TINY)
        entry = matern(work[first:last]).reshape((last - first) // RHS, RHS, COLS) - mid[tile][None]
        entry = entry.reshape(last - first, COLS).astype(BF16)
        rowacc[:, first:last] += lax.dot_general(
            bbuf[tile, :HEAD, :], entry, (((1,), (1,)), ((), ())), preferred_element_type=F32
        )
        return both(jnp.dot(va[kind, :, first:last], entry, preferred_element_type=F32))

    def add_constant(tile, *parts):
        constant = both(bbuf[tile, :HEAD, :].astype(F32)) * mid[tile]
        for part in parts:
            corr[part] += constant

    def first_part(tile):
        add_columns(tile)
        add_constant(tile, 0, 1, 2, 3)
        colacc[tile] = run_part(tile, 0, PART, 0) + wsum[0] * mid[tile]

    def second_part(tile):
        colacc[tile] += run_part(tile, PART, ROWS, 0) + wsum[1] * mid[tile]

    def whole_tile(tile):
        add_columns(tile)
        add_constant(tile, 0, 1, 2, 3)
        colacc[tile] = run_part(tile, 0, ROWS, 0) + (wsum[0] + wsum[1]) * mid[tile]

    def end_tile(tile):
        add_columns(tile)
        add_constant(tile, 0, 2)
        col = run_part(tile, 0, ENDS[0], 1) + run_part(tile, PART, ENDS[1], 1)
        colacc[tile] = col + wsum[2] * mid[tile]

    def send_columns(tile):
        total = colacc[tile]
        cmsg[tile, 0] = total[:, :PTS]
        cmsg[tile, 1] = total[:, PTS:]
        col_copy(tile, 0).start()
        col_copy(tile, 1).start()

    def early(tile, _):
        @pl.when((tile > 1) & (tile < 4))
        def _():
            fetch(tile + 1)

        @pl.when(tile == 4)
        def _():
            fetch(RELAY)
            line_copy(8, RELAY, -2).start()
            line_copy(7, RELAY, -1).start()
            line_copy(5, RELAY, 1).start()

        sib_copy(tile).wait_recv()
        first_part(tile)
        return 0

    lax.fori_loop(1, 5, early, 0)

    for k in range(NEAR, PLACES):
        plane_copy(k).wait_recv()
    for k in range(NEAR, PLACES):
        add_rows(k)
    wsum[1] = spread(va[0, :, PART:].astype(F32))
    k_of = lax.div(lax.broadcasted_iota(jnp.int32, (HEAD, ROWS), 1), PTS)
    once = k_of * PTS < ENDS[0]
    once = once | ((k_of >= NEAR) & (k_of * PTS < ENDS[1]))
    for k in LONE:
        once = once & (k_of != k)
    masked = jnp.where(once, va[0].astype(F32), 0.0)
    va[1] = masked.astype(BF16)
    wsum[2] = spread(masked)

    def late(index, order):
        tile = lax.rem(order, 9)
        order = order // 9
        after = lax.rem(order, 9)

        @pl.when((after == 5) | (after > RELAY))
        def _():
            fetch(after)

        @pl.when((tile == 0) | (tile > 4))
        def _():
            sib_copy(tile).wait_recv()

        @pl.when((tile == 0) | (tile == HALF))
        def _():
            end_tile(tile)

        @pl.when((tile > 4) & (tile < HALF))
        def _():
            whole_tile(tile)

        @pl.when((tile > 0) & (tile < 5))
        def _():
            second_part(tile)

        @pl.when(tile > 0)
        def _():
            send_columns(tile)

        return order

    third, quarter = lax.div(plane, 8), lax.div(plane, 12)
    order = ORDERS[0] + third * (ORDERS[1] - ORDERS[0]) + quarter * (ORDERS[2] - ORDERS[1])
    lax.fori_loop(0, HALF + 1, late, order)

    for k in range(PLACES):
        part = 2 * (k >= NEAR) + (k * PTS >= ENDS[0] if k < NEAR else k * PTS >= ENDS[1])
        rmsg[k] = both(rowacc[:, k * PTS : (k + 1) * PTS]) + jnp.sum(corr[part], axis=1, keepdims=True)
        if k:
            row_copy(k).start()
    cmsg[0, 1] = colacc[0, :, PTS:]
    col_copy(0, 1).start()

    total = rmsg[0] + colacc[0, :, :PTS]
    for tile in range(HALF + 1):
        for other in range(2):
            if tile or other:
                col_copy(tile, other).wait_recv()
                total += crecv[tile, other]
    for k in range(1, PLACES):
        row_copy(k).wait_recv()
        total += rrecv[k]
    out_ref[...] = total * SCALE

    for tile in range(HALF + 1):
        sib_copy(tile).wait_send()
        if tile:
            line_copy(tile).wait_send()
            col_copy(tile, 0).wait_send()
        col_copy(tile, 1).wait_send()
    for k in range(1, PLACES):
        plane_copy(k).wait_send()
        row_copy(k).wait_send()


def body(features, inv_length, vectors):
    dma = pltpu.SemaphoreType.DMA
    return pl.pallas_call(
        kernel,
        out_shape=jax.ShapeDtypeStruct((RHS, PTS), F32),
        in_specs=[pl.BlockSpec(memory_space=pltpu.HBM)] * 3,
        out_specs=pl.BlockSpec(memory_space=pltpu.VMEM),
        scratch_shapes=[
            pltpu.VMEM((PTS, FEAT), F32),
            pltpu.VMEM((1, FEAT), F32),
            pltpu.VMEM((RHS, PTS), F32),
            pltpu.VMEM((PLACES, PTS + HEAD, FEAT), BF16),
            pltpu.VMEM((HALF + 1, HEAD + FEAT + AUG, COLS), BF16),
            pltpu.VMEM((ROWS, 2 * FEAT), BF16),
            pltpu.VMEM((2, HEAD, ROWS), BF16),
            pltpu.VMEM((HEAD, ROWS), F32),
            pltpu.VMEM((4, RHS, COLS), F32),
            pltpu.VMEM((ROWS, COLS), F32),
            pltpu.VMEM((HEAD, 2 * FEAT), BF16),
            pltpu.VMEM((HALF + 1, RHS, COLS), F32),
            pltpu.VMEM((3, RHS, COLS), F32),
            pltpu.VMEM((HALF + 1, RHS, COLS), F32),
            pltpu.VMEM((HALF + 1, 2, RHS, PTS), F32),
            pltpu.VMEM((PLACES, RHS, PTS), F32),
            pltpu.VMEM((PLACES, RHS, PTS), F32),
            pltpu.VMEM((HALF + 1, 2, RHS, PTS), F32),
            dma((3,)),
            dma((PLACES,)), dma((PLACES,)),
            dma((HALF + 1,)), dma((HALF + 1,)),
            dma((HALF + 1,)), dma((HALF + 1,)),
            dma((PLACES,)), dma((PLACES,)),
            dma((HALF + 1, 2)), dma((HALF + 1, 2)),
        ],
        compiler_params=pltpu.CompilerParams(
            collective_id=0, has_side_effects=True, vmem_limit_bytes=60 * 2**20
        ),
        name="matern",
    )(features, inv_length.reshape(1, FEAT), vectors)


def solution(mesh):
    return jax.shard_map(
        body,
        mesh=mesh,
        in_specs=(P(("blk", "wide"), None), P(), P(None, ("blk", "wide"))),
        out_specs=P(None, ("blk", "wide")),
        check_vma=False,
    )
```

```python
import jax
import jax.numpy as jnp
from jax import lax
from jax.experimental import pallas as pl
from jax.experimental.pallas import tpu as pltpu
from jax.sharding import PartitionSpec as P

MESH = pl.DeviceIdType.MESH
F32, BF16 = jnp.float32, jnp.bfloat16

PTS = 128
FEAT = 128
RHS = 8
PLANES = 16
HALF = 8
HEAD = 2 * RHS
AUG = 16
COLS = 2 * PTS
RELAY = 6

SLOTS = (
    (0, 0), (1, 0), (0, 1), (1, 1), (1, -1), (-1, 0), (0, -1), (-1, -1), (-1, 1),
    (2, 0), (0, 2), (2, 2), (1, 2), (2, 1), (-1, 2), (2, -1),
)
PLACES = len(SLOTS)
NEAR = 9
LONE = (0, 9, 10, 11)
PASSED = ((11, 7, (-1, -1)), (15, 7, (-1, 0)), (14, 7, (0, -1)), (13, 3, (1, 0)), (12, 3, (0, 1)), (9, 1, (1, 0)), (10, 2, (0, 1)))
ROWS = PLACES * PTS
PART = NEAR * PTS
ENDS = (5 * PTS, 14 * PTS)


def packed(*tiles):
    return sum(tile * 9**i for i, tile in enumerate(tiles))


ORDERS = (packed(1, 2, 3, 4, 6, 5, 7, 8, 0), packed(1, 2, 6, 8, 7, 5, 3, 4, 0), packed(1, 2, 6, 5, 7, 8, 3, 4, 0))

SCALE = 5.0 / 3.0
ALPHA = 3.0 / 5.0**0.5
BETA = 0.6
DECAY = -(5.0**0.5) * 1.4426950408889634
TINY = 1e-30


def step_of(tile):
    return tile * (2 * ((tile + 3) // 8) - 1)


def split3(value):
    high = value.astype(BF16)
    rest = value - high.astype(F32)
    mid = rest.astype(BF16)
    low = (rest - mid.astype(F32)).astype(BF16)
    return high.astype(F32), mid.astype(F32), low.astype(F32)


def matern(dist2):
    r = dist2 * lax.rsqrt(dist2)
    return ((r + ALPHA) * r + BETA) * jnp.exp2(r * DECAY)


def kernel(
    feat_hbm, inv_hbm, vec_hbm, out_ref,
    feat_ref, inv_ref, vec_ref, abuf, bbuf, amat, va, rowacc, corr, work, mean, mid, wsum, colacc, cmsg, rmsg, rrecv, crecv,
    in_sem, plane_send, plane_recv, line_send, line_recv, sib_send, sib_recv, row_send, row_recv, col_send, col_recv,
):
    loads = [
        pltpu.make_async_copy(src, dst, in_sem.at[i])
        for i, (src, dst) in enumerate(((feat_hbm, feat_ref), (inv_hbm, inv_ref), (vec_hbm, vec_ref)))
    ]
    for load in loads:
        load.start()

    blk, wide = lax.axis_index("blk"), lax.axis_index("wide")
    core = lax.rem(blk, 2)
    x_here = 2 * lax.div(blk, HALF) + lax.div(wide, PLANES)
    y_here = lax.rem(lax.div(blk, 2), 4)
    plane = lax.rem(wide, PLANES)

    def device(dz, offset, other):
        x, y = lax.rem(x_here + offset[0] + 4, 4), lax.rem(y_here + offset[1] + 4, 4)
        z = lax.rem(plane + dz + PLANES, PLANES)
        c = 1 - core if other else core
        return {"blk": lax.div(x, 2) * HALF + y * 2 + c, "wide": lax.rem(x, 2) * PLANES + z}

    def back(offset):
        return (-offset[0], -offset[1])

    def plane_copy(k, source=0, offset=(0, 0)):
        return pltpu.make_async_remote_copy(
            src_ref=abuf.at[source], dst_ref=abuf.at[k], send_sem=plane_send.at[k], recv_sem=plane_recv.at[k],
            device_id=device(0, offset, False), device_id_type=MESH,
        )

    def pass_on(source):
        for k, at, offset in PASSED:
            if at == source:
                plane_copy(k, source, back(offset)).start()

    def line_copy(tile, source=0, hops=0):
        return pltpu.make_async_remote_copy(
            src_ref=bbuf.at[source, :, :PTS], dst_ref=bbuf.at[tile, :, :PTS],
            send_sem=line_send.at[tile], recv_sem=line_recv.at[tile],
            device_id=device(hops, (0, 0), False), device_id_type=MESH,
        )

    def sib_copy(tile):
        return pltpu.make_async_remote_copy(
            src_ref=bbuf.at[tile, :, :PTS], dst_ref=bbuf.at[tile, :, PTS:],
            send_sem=sib_send.at[tile], recv_sem=sib_recv.at[tile],
            device_id=device(0, (0, 0), True), device_id_type=MESH,
        )

    def row_copy(k):
        return pltpu.make_async_remote_copy(
            src_ref=rmsg.at[k], dst_ref=rrecv.at[k], send_sem=row_send.at[k], recv_sem=row_recv.at[k],
            device_id=device(0, SLOTS[k], False), device_id_type=MESH,
        )

    def col_copy(tile, other):
        return pltpu.make_async_remote_copy(
            src_ref=cmsg.at[tile, other], dst_ref=crecv.at[tile, other],
            send_sem=col_send.at[tile, other], recv_sem=col_recv.at[tile, other],
            device_id=device(step_of(tile), (0, 0), other == 1), device_id_type=MESH,
        )

    barrier = pltpu.get_barrier_semaphore()
    for dz in (RELAY, 2, -2, 1, -1):
        pl.semaphore_signal(barrier, inc=1, device_id=device(dz, (0, 0), False), device_id_type=MESH)
    for k in range(1, NEAR):
        pl.semaphore_signal(barrier, inc=1, device_id=device(0, SLOTS[k], False), device_id_type=MESH)
    pl.semaphore_signal(barrier, inc=1, device_id=device(0, (0, 0), True), device_id_type=MESH)

    for load in loads:
        load.wait()
    scaled = (feat_ref[...] * inv_ref[...]).astype(BF16).astype(F32)
    vec = vec_ref[...]
    vec_high = vec.astype(BF16).astype(F32)
    head = jnp.concatenate([vec_high, vec - vec_high], axis=0).astype(BF16)
    abuf[0, :PTS, :] = (scaled * -2.0).astype(BF16)
    abuf[0, PTS:, :] = head
    bbuf[0, :HEAD, :PTS] = head
    turned = scaled.T
    bbuf[0, HEAD : HEAD + FEAT, :PTS] = turned.astype(BF16)
    n0, n1, n2 = split3(jnp.sum(turned * turned, axis=0, keepdims=True))
    sub = lax.broadcasted_iota(jnp.int32, (AUG, PTS), 0)
    extra = jnp.where(sub < 3, 1.0, jnp.where(sub == 3, n0, jnp.where(sub == 4, n1, jnp.where(sub == 5, n2, 0.0))))
    bbuf[0, HEAD + FEAT :, :PTS] = extra.astype(BF16)

    pl.semaphore_wait(barrier, NEAR - 1 + 5 + 1)

    line_copy(RELAY, 0, -RELAY).start()
    line_copy(2, 0, 2).start()
    for k in (7, 3, 1, 2):
        plane_copy(k, 0, back(SLOTS[k])).start()
    line_copy(1, 0, 1).start()
    sib_copy(0).start()
    for k in (4, 5, 6, 8):
        plane_copy(k, 0, back(SLOTS[k])).start()

    lane = lax.broadcasted_iota(jnp.int32, (PTS, PTS), 1)
    ones = jnp.ones((2 * FEAT, PTS), BF16)

    def add_rows(k):
        at = k * PTS
        points = abuf[k, :PTS, :]
        wide_points = points.astype(F32)
        square = wide_points * wide_points
        high = square.astype(BF16)
        low = (square - high.astype(F32)).astype(BF16)
        norm = 0.25 * jnp.dot(jnp.concatenate([high, low], axis=1), ones, preferred_element_type=F32)
        n0, n1, n2 = split3(norm)
        extra = jnp.where(lane == 0, n0, jnp.where(lane == 1, n1, jnp.where(lane == 2, n2, jnp.where(lane < 6, 1.0, 0.0))))
        amat[at : at + PTS, :FEAT] = points
        amat[at : at + PTS, FEAT:] = extra.astype(BF16)
        va[0, :, at : at + PTS] = abuf[k, PTS:, :]

    def fetch(tile):
        line_copy(tile).wait_recv()
        sib_copy(tile).start()

    add_rows(0)
    rowacc[...] = jnp.zeros_like(rowacc)
    corr[...] = jnp.zeros_like(corr)
    for k in (7, 3, 1, 2):
        plane_copy(k).wait_recv()
        pass_on(k)
    for k in (7, 3, 1, 2):
        add_rows(k)
    fetch(1)
    fetch(2)
    line_copy(4, 2, 2).start()
    line_copy(3, 2, 1).start()
    for k in (4, 5, 6, 8):
        plane_copy(k).wait_recv()
    for k in (4, 5, 6, 8):
        add_rows(k)

    def both(value):
        return value[:RHS] + value[RHS:]

    def spread(value):
        return jnp.broadcast_to(jnp.sum(both(value), axis=1, keepdims=True), (RHS, COLS))

    wsum[0] = spread(va[0, :, :PART].astype(F32))
    mean[...] = jnp.dot(jnp.full((HEAD, PART), 1.0 / PART, BF16), amat[:PART], preferred_element_type=F32).astype(BF16)

    def add_columns(tile):
        mid[tile] = matern(jnp.maximum(jnp.dot(mean[:, : FEAT + AUG], bbuf[tile, HEAD:, :], preferred_element_type=F32)[:RHS], TINY))

    def run_part(tile, first, last, kind):
        right = bbuf[tile, HEAD:, :]
        dist2 = jnp.dot(amat[first:last, : FEAT + AUG], right, preferred_element_type=F32)
        work[first:last] = jnp.maximum(dist2, TINY)
        entry = matern(work[first:last]).reshape((last - first) // RHS, RHS, COLS) - mid[tile][None]
        entry = entry.reshape(last - first, COLS).astype(BF16)
        rowacc[:, first:last] += lax.dot_general(
            bbuf[tile, :HEAD, :], entry, (((1,), (1,)), ((), ())), preferred_element_type=F32
        )
        return both(jnp.dot(va[kind, :, first:last], entry, preferred_element_type=F32))

    def add_constant(tile, *parts):
        constant = both(bbuf[tile, :HEAD, :].astype(F32)) * mid[tile]
        for part in parts:
            corr[part] += constant

    def first_part(tile):
        add_columns(tile)
        add_constant(tile, 0, 1, 2, 3)
        colacc[tile] = run_part(tile, 0, PART, 0) + wsum[0] * mid[tile]

    def second_part(tile):
        colacc[tile] += run_part(tile, PART, ROWS, 0) + wsum[1] * mid[tile]

    def whole_tile(tile):
        add_columns(tile)
        add_constant(tile, 0, 1, 2, 3)
        colacc[tile] = run_part(tile, 0, ROWS, 0) + (wsum[0] + wsum[1]) * mid[tile]

    def end_tile(tile):
        add_columns(tile)
        add_constant(tile, 0, 2)
        col = run_part(tile, 0, ENDS[0], 1) + run_part(tile, PART, ENDS[1], 1)
        colacc[tile] = col + wsum[2] * mid[tile]

    def send_columns(tile):
        total = colacc[tile]
        cmsg[tile, 0] = total[:, :PTS]
        cmsg[tile, 1] = total[:, PTS:]
        col_copy(tile, 0).start()
        col_copy(tile, 1).start()

    def early(tile, _):
        @pl.when((tile > 1) & (tile < 4))
        def _():
            fetch(tile + 1)

        @pl.when(tile == 4)
        def _():
            fetch(RELAY)
            line_copy(8, RELAY, -2).start()
            line_copy(7, RELAY, -1).start()
            line_copy(5, RELAY, 1).start()

        sib_copy(tile).wait_recv()
        first_part(tile)
        return 0

    lax.fori_loop(1, 5, early, 0)

    for k in range(NEAR, PLACES):
        plane_copy(k).wait_recv()
    for k in range(NEAR, PLACES):
        add_rows(k)
    wsum[1] = spread(va[0, :, PART:].astype(F32))
    k_of = lax.div(lax.broadcasted_iota(jnp.int32, (HEAD, ROWS), 1), PTS)
    once = k_of * PTS < ENDS[0]
    once = once | ((k_of >= NEAR) & (k_of * PTS < ENDS[1]))
    for k in LONE:
        once = once & (k_of != k)
    masked = jnp.where(once, va[0].astype(F32), 0.0)
    va[1] = masked.astype(BF16)
    wsum[2] = spread(masked)

    def late(index, order):
        tile = lax.rem(order, 9)
        order = order // 9
        after = lax.rem(order, 9)

        @pl.when((after == 5) | (after > RELAY))
        def _():
            fetch(after)

        @pl.when((tile == 0) | (tile > 4))
        def _():
            sib_copy(tile).wait_recv()

        @pl.when((tile == 0) | (tile == HALF))
        def _():
            end_tile(tile)

        @pl.when((tile > 4) & (tile < HALF))
        def _():
            whole_tile(tile)

        @pl.when((tile > 0) & (tile < 5))
        def _():
            second_part(tile)

        @pl.when(tile > 0)
        def _():
            send_columns(tile)

        return order

    third, quarter = lax.div(plane, 8), lax.div(plane, 12)
    order = ORDERS[0] + third * (ORDERS[1] - ORDERS[0]) + quarter * (ORDERS[2] - ORDERS[1])
    lax.fori_loop(0, HALF + 1, late, order)

    for k in range(PLACES):
        part = 2 * (k >= NEAR) + (k * PTS >= ENDS[0] if k < NEAR else k * PTS >= ENDS[1])
        rmsg[k] = both(rowacc[:, k * PTS : (k + 1) * PTS]) + jnp.sum(corr[part], axis=1, keepdims=True)
        if k:
            row_copy(k).start()
    cmsg[0, 1] = colacc[0, :, PTS:]
    col_copy(0, 1).start()

    total = rmsg[0] + colacc[0, :, :PTS]
    for tile in range(HALF + 1):
        for other in range(2):
            if tile or other:
                col_copy(tile, other).wait_recv()
                total += crecv[tile, other]
    for k in range(1, PLACES):
        row_copy(k).wait_recv()
        total += rrecv[k]
    out_ref[...] = total * SCALE

    for tile in range(HALF + 1):
        sib_copy(tile).wait_send()
        if tile:
            line_copy(tile).wait_send()
            col_copy(tile, 0).wait_send()
        col_copy(tile, 1).wait_send()
    for k in range(1, PLACES):
        plane_copy(k).wait_send()
        row_copy(k).wait_send()


def body(features, inv_length, vectors):
    dma = pltpu.SemaphoreType.DMA
    return pl.pallas_call(
        kernel,
        out_shape=jax.ShapeDtypeStruct((RHS, PTS), F32),
        in_specs=[pl.BlockSpec(memory_space=pltpu.HBM)] * 3,
        out_specs=pl.BlockSpec(memory_space=pltpu.VMEM),
        scratch_shapes=[
            pltpu.VMEM((PTS, FEAT), F32),
            pltpu.VMEM((1, FEAT), F32),
            pltpu.VMEM((RHS, PTS), F32),
            pltpu.VMEM((PLACES, PTS + HEAD, FEAT), BF16),
            pltpu.VMEM((HALF + 1, HEAD + FEAT + AUG, COLS), BF16),
            pltpu.VMEM((ROWS, 2 * FEAT), BF16),
            pltpu.VMEM((2, HEAD, ROWS), BF16),
            pltpu.VMEM((HEAD, ROWS), F32),
            pltpu.VMEM((4, RHS, COLS), F32),
            pltpu.VMEM((ROWS, COLS), F32),
            pltpu.VMEM((HEAD, 2 * FEAT), BF16),
            pltpu.VMEM((HALF + 1, RHS, COLS), F32),
            pltpu.VMEM((3, RHS, COLS), F32),
            pltpu.VMEM((HALF + 1, RHS, COLS), F32),
            pltpu.VMEM((HALF + 1, 2, RHS, PTS), F32),
            pltpu.VMEM((PLACES, RHS, PTS), F32),
            pltpu.VMEM((PLACES, RHS, PTS), F32),
            pltpu.VMEM((HALF + 1, 2, RHS, PTS), F32),
            dma((3,)),
            dma((PLACES,)), dma((PLACES,)),
            dma((HALF + 1,)), dma((HALF + 1,)),
            dma((HALF + 1,)), dma((HALF + 1,)),
            dma((PLACES,)), dma((PLACES,)),
            dma((HALF + 1, 2)), dma((HALF + 1, 2)),
        ],
        compiler_params=pltpu.CompilerParams(
            collective_id=0, has_side_effects=True, vmem_limit_bytes=60 * 2**20
        ),
        name="matern",
    )(features, inv_length.reshape(1, FEAT), vectors)


def solution(mesh):
    return jax.shard_map(
        body,
        mesh=mesh,
        in_specs=(P(("blk", "wide"), None), P(), P(None, ("blk", "wide"))),
        out_specs=P(None, ("blk", "wide")),
        check_vma=False,
    )
```
